32 devices in a mesh: dp: 8 (over z, y), seq: 4 (over x, core).
Axes of the slice: x: 2, y: 2, z: 4, core: 2. Of those that a mesh axis runs over, the one named last changes fastest.
Arguments:
- query_rows: bfloat16 [4096, 3072], P(('dp', 'seq')), may hold values from -2000 to 2000
- key_rows: bfloat16 [4096, 3072], P(('dp', 'seq')), may hold values from -2000 to 2000
- value_rows: bfloat16 [4096, 3072], P(('dp', 'seq')), may hold values from -6 to 6
- output_grad: bfloat16 [4096, 3072], P(('dp', 'seq')), may hold values from -6 to 6
- query_gain: float32 [128], replicated, may hold values from 0.5 to 5
- key_gain: float32 [128], replicated, may hold values from 0.5 to 5
- dest_groups: int32 [32, 8], P(('dp', 'seq')), may hold values from 0 to 7, each once within a row
- slot_sources: int32 [8, 32], P('dp'), may hold values from 0 to 31, each once within a row
- clip_index: int32 [8, 512], P('dp'), may hold values from 0 to 1, never falling along the last dimension, each value on 1 to 384 neighbouring positions
Outputs:
- attended: bfloat16 [4096, 3072], P(('dp', 'seq'))
- query_grad: bfloat16 [4096, 3072], P(('dp', 'seq'))
- key_grad: bfloat16 [4096, 3072], P(('dp', 'seq'))
- value_grad: bfloat16 [4096, 3072], P(('dp', 'seq'))
- gain_grads: float32 [2, 128], replicated
The draws below stay inside these ranges and needn't reach their ends.
Inputs may be any that keep to these rules, and one draw needn't show every extreme that they name: `dest_groups`: each row names every group once. `slot_sources`: each row names every device once. `clip_index`: clip numbers never fall along a group's sequence; in each group one clip covers 128 to 384 positions and the other the rest.
All inputs are finite; a program needn't handle non-finite values.
Results may differ from the reference program's by a relative error of at most 0.003.
The reference program's roundings to bfloat16 on the way count: a program that leaves them out, or rounds other values in their place, can miss the bound.
Values may be sent and summed in bfloat16 or wider, within the bound.
A program may use at most 128 MiB of HBM per device.

```python
import math
import jax
import jax.numpy as jnp
import numpy as np
from jax import lax

D = 3072
HEADS = 24
HD = 128
TOK_DEV = 128
CLIPS = 2
GROUP_TOK = 512
SOURCES = 32
TOKENS = 4096
N_DP = 8


def shared_pair(base_key, aligned):
    width = HEADS * HD
    seeds = [jax.random.fold_in(base_key, 101 + number) for number in range(9)]
    ten_log = math.log(10.0)
    query_rowscale = jnp.exp(jax.random.uniform(seeds[0], (TOKENS, 1), jnp.float32, 0.0, ten_log))
    query_colscale = jnp.exp(jax.random.uniform(seeds[1], (1, width), jnp.float32, 0.0, ten_log))
    key_rowscale = jnp.exp(jax.random.uniform(seeds[2], (TOKENS, 1), jnp.float32, 0.0, ten_log))
    key_colscale = jnp.exp(jax.random.uniform(seeds[3], (1, width), jnp.float32, 0.0, ten_log))
    query_base = jnp.clip(jax.random.normal(seeds[4], (TOKENS, width), jnp.float32), -5.0, 5.0) * query_rowscale * query_colscale
    key_base = jnp.clip(jax.random.normal(seeds[5], (TOKENS, width), jnp.float32), -5.0, 5.0) * key_rowscale * key_colscale
    row_ids = jnp.arange(TOKENS)
    leader = (row_ids % 8 == 0).astype(jnp.float32)[:, None]
    follower = (row_ids % 8 == 1).astype(jnp.float32)[:, None]
    key_out = key_base * (1.0 - aligned * follower)
    query_out = query_base * (1.0 - aligned * leader)
    return (query_out, key_out)


def draw_query_rows(key, part):
    paired = shared_pair(key, 0.0)
    return paired[0].astype(jnp.bfloat16)


def draw_key_rows(key, part):
    paired = shared_pair(key, 0.0)
    return paired[1].astype(jnp.bfloat16)


def draw_query_gain(key, part):
    key = jax.random.fold_in(key, 7)
    return jnp.exp(jax.random.uniform(key, (HD,), jnp.float32, math.log(0.5), math.log(2.0)))


def draw_key_gain(key, part):
    key = jax.random.fold_in(key, 9)
    return jnp.exp(jax.random.uniform(key, (HD,), jnp.float32, math.log(0.5), math.log(2.0)))


def block_levels(key, shape, cuts, smallest, largest):
    def one(dim, shards_of):
        heights = jax.random.uniform(jax.random.fold_in(jax.random.fold_in(key, 6), dim), (shards_of,), jnp.float32, smallest / len(cuts), largest / len(cuts))
        return jnp.repeat(jnp.exp(heights), shape[dim] // shards_of).reshape((-1,) + (1,) * (len(shape) - dim - 1))

    loudness = one(*cuts[0])
    for cut in cuts[1:]:
        loudness = loudness * one(*cut)
    return loudness


def profile(number_of, total, reach, slope):
    portions = [(1 << 20) // math.isqrt(rank ** slope) + 1 for rank in range(2, number_of + 1)]
    surplus, given = total - reach - (number_of - 1), [1] * (number_of - 1)
    while surplus > 0:
        movable = [i for i in range(number_of - 1) if given[i] < reach]
        whole, remaining = sum([portions[i] for i in movable]), surplus
        for i in movable:
            addition = min(reach - given[i], max(1, remaining * portions[i] // whole), surplus)
            given[i] = given[i] + addition
            surplus = surplus - addition
    return np.array([reach] + given)


def uneven(key, count, total, most, skew):
    if count == 2:
        one = jax.random.randint(key, (), max(1, total - most), min(most, total - 1) + 1)
        return jnp.stack([one, total - one])
    tallies = jnp.asarray(profile(count, total, most, skew), jnp.int32)
    twos = (count - 1) // 2
    giver, receiver = tallies[1:1 + 2 * twos:2], tallies[2:2 + 2 * twos:2]
    margin = jnp.minimum(giver - 1, most - receiver)
    shifted = jax.random.randint(jax.random.fold_in(key, 1), (twos,), 0, 1 << 20) % (margin + 1)
    tallies = tallies.at[1:1 + 2 * twos:2].set(giver - shifted).at[2:2 + 2 * twos:2].set(receiver + shifted)
    return tallies[jax.random.permutation(jax.random.fold_in(key, 2), count)]


def centred(key, dims, scale, reach, split=(), kind=jnp.bfloat16):
    entries = scale * jax.random.normal(key, dims, jnp.float32)
    if split:
        entries = entries * block_levels(key, dims, split, -0.22, 0.18)
    return jnp.clip(entries, -reach, reach).astype(kind)


def setup_inputs(seed: int = 0) -> dict:
    key_of = jax.random.split(jax.random.key(seed), 10)
    query_rows = draw_query_rows(jax.random.fold_in(key_of[9], 71), 0)
    key_rows = draw_key_rows(jax.random.fold_in(key_of[9], 71), 0)
    value_rows = centred(key_of[2], (TOKENS, D), 1.0, 6.0, ((0, 32),))
    output_grad = centred(key_of[3], (TOKENS, D), 1.0, 6.0, ((0, 32),))
    query_gain = draw_query_gain(jax.random.fold_in(key_of[9], 71), 0)
    key_gain = draw_key_gain(jax.random.fold_in(key_of[9], 71), 0)
    dest_groups = jax.vmap(lambda own: jax.random.permutation(own, N_DP))(jax.random.split(key_of[6], SOURCES)).reshape((SOURCES, N_DP)).astype(jnp.int32)
    slot_sources = jax.vmap(lambda own: jax.random.permutation(own, SOURCES))(jax.random.split(key_of[7], N_DP)).reshape((N_DP, SOURCES)).astype(jnp.int32)
    clip_index = jax.vmap(lambda own: jnp.searchsorted(jnp.cumsum(uneven(own, CLIPS, GROUP_TOK, GROUP_TOK * 3 // 4, 2)), jnp.arange(GROUP_TOK), side="right"))(jax.random.split(key_of[8], N_DP)).reshape((N_DP, GROUP_TOK)).astype(jnp.int32)
    return dict(query_rows=query_rows, key_rows=key_rows, value_rows=value_rows, output_grad=output_grad, query_gain=query_gain, key_gain=key_gain, dest_groups=dest_groups, slot_sources=slot_sources, clip_index=clip_index)


EPS = 1e-06

def norm_forward(tensor, gain_vec):
    inverse = lax.rsqrt(lax.optimization_barrier(jnp.mean(tensor * tensor, axis=-1, keepdims=True)) + EPS)
    return (inverse, (tensor * inverse * gain_vec).astype(jnp.bfloat16))

def norm_backward(tensor, inverse, gain_vec, upstream):
    inner_mean = lax.optimization_barrier(jnp.mean(gain_vec * upstream * tensor, axis=-1, keepdims=True))
    grad_input = inverse * gain_vec * upstream - tensor * inverse ** 3 * inner_mean
    grad_gain = lax.optimization_barrier(jnp.sum(upstream * tensor * inverse, axis=(0, 1)))
    return (grad_input.astype(jnp.bfloat16), grad_gain)

def group_attention(queries, keys_in, values_in, grads_in, clip_row, query_gain, key_gain):
    score_scale = HD ** (-0.5)
    query_wide = queries.astype(jnp.float32)
    key_wide = keys_in.astype(jnp.float32)
    query_inv, query_norm = norm_forward(query_wide, query_gain)
    key_inv, key_norm = norm_forward(key_wide, key_gain)
    scores = jnp.einsum('qhd,khd->hqk', query_norm.astype(jnp.float32), key_norm.astype(jnp.float32)) * score_scale
    same_clip = (clip_row[:, None] == clip_row[None, :])[None]
    masked = jnp.where(same_clip, scores, -1e+30)
    row_top = lax.optimization_barrier(jnp.max(masked, axis=-1, keepdims=True))
    weights = jnp.where(same_clip, jnp.exp(masked - row_top), 0.0)
    probs_full = weights / lax.optimization_barrier(jnp.sum(weights, axis=-1, keepdims=True))
    probs_low = probs_full.astype(jnp.bfloat16)
    value_wide = values_in.astype(jnp.float32)
    grads_wide = grads_in.astype(jnp.float32)
    attended = jnp.einsum('hqk,khd->qhd', probs_low.astype(jnp.float32), value_wide)
    value_grad = jnp.einsum('hqk,qhd->khd', probs_low.astype(jnp.float32), grads_wide).astype(jnp.bfloat16)
    prob_grad = jnp.einsum('qhd,khd->hqk', grads_wide, value_wide)
    row_delta = lax.optimization_barrier(jnp.sum(grads_wide * attended, axis=-1)).T[:, :, None]
    score_grad = (probs_full * (prob_grad - row_delta) * score_scale).astype(jnp.bfloat16)
    query_grad_norm = jnp.einsum('hqk,khd->qhd', score_grad.astype(jnp.float32), key_norm.astype(jnp.float32))
    key_grad_norm = jnp.einsum('hqk,qhd->khd', score_grad.astype(jnp.float32), query_norm.astype(jnp.float32))
    query_grad, query_gain_grad = norm_backward(query_wide, query_inv, query_gain, query_grad_norm)
    key_grad, key_gain_grad = norm_backward(key_wide, key_inv, key_gain, key_grad_norm)
    return (attended.astype(jnp.bfloat16), query_grad, key_grad, value_grad, query_gain_grad, key_gain_grad)

def reference(query_rows, key_rows, value_rows, output_grad, query_gain, key_gain, dest_groups, slot_sources, clip_index):
    block_rows = TOK_DEV // N_DP
    group_ids = jnp.arange(N_DP, dtype=jnp.int32)
    position = lax.optimization_barrier(jnp.sum(jnp.where(dest_groups[:, None, :] == group_ids[None, :, None], group_ids[None, None, :], 0), axis=2)).astype(jnp.int32)
    offsets = jnp.arange(block_rows, dtype=jnp.int32)

    def rows_of(group_index):
        source_list = slot_sources[group_index]
        starts = source_list * TOK_DEV + position[source_list, group_index] * block_rows
        return (starts[:, None] + offsets[None, :]).reshape(-1).astype(jnp.int32)
    row_table = jax.vmap(rows_of)(group_ids)

    def one_group(group_index):
        row_list = row_table[group_index]

        def select(tensor):
            return jnp.take(tensor, row_list, axis=0).reshape(GROUP_TOK, HEADS, HD)
        return group_attention(select(query_rows), select(key_rows), select(value_rows), select(output_grad), clip_index[group_index], query_gain, key_gain)
    results = lax.map(one_group, group_ids)
    flat_rows = row_table.reshape(-1)

    def scatter_home(tensor):
        return jnp.zeros((TOKENS, HEADS * HD), jnp.bfloat16).at[flat_rows].set(tensor.reshape(-1, HEADS * HD))
    factor = (TOKENS * HEADS) ** (-0.5)
    gain_grads = jnp.stack([lax.optimization_barrier(jnp.sum(results[4], axis=0)), lax.optimization_barrier(jnp.sum(results[5], axis=0))]) * factor
    return (scatter_home(results[0]), scatter_home(results[1]), scatter_home(results[2]), scatter_home(results[3]), gain_grads)
```

```python
import functools

import jax
import jax.numpy as jnp
from jax import lax
from jax.experimental import pallas as pl
from jax.experimental.pallas import tpu as pltpu
from jax.sharding import PartitionSpec as P

EPS = 1e-06


def norm_forward(tensor, gain_vec):
    inverse = lax.rsqrt(jnp.mean(tensor * tensor, axis=-1, keepdims=True) + EPS)
    return (inverse, (tensor * inverse * gain_vec).astype(jnp.bfloat16))


def norm_backward(tensor, inverse, gain_vec, upstream):
    inner_mean = jnp.mean(gain_vec * upstream * tensor, axis=-1, keepdims=True)
    grad_input = inverse * gain_vec * upstream - tensor * inverse**3 * inner_mean
    grad_gain = jnp.sum(upstream * tensor * inverse, axis=(0, 1))
    return (grad_input.astype(jnp.bfloat16), grad_gain)


def shards_plain(
    query_rows,
    key_rows,
    value_rows,
    output_grad,
    query_gain,
    key_gain,
    dest_groups,
    slot_sources,
    clip_index,
):
    group_count = lax.axis_size("dp")
    head_ways = lax.axis_size("seq")
    tok_rows, full_width = query_rows.shape
    head_size = query_gain.shape[0]
    heads_total = full_width // head_size
    heads_here = heads_total // head_ways
    span_width = heads_here * head_size
    block_rows = tok_rows // group_count
    source_count = group_count * head_ways
    seq_rows = tok_rows * head_ways
    targets = dest_groups[0]
    group_ids = jnp.arange(group_count, dtype=jnp.int32)
    block_order = jnp.sum(
        jnp.where(targets[None, :] == group_ids[:, None], group_ids[None, :], 0), axis=1
    )

    def pack_out(tensor):
        blocks = tensor.reshape(group_count, block_rows, head_ways, span_width)
        return jnp.take(blocks, block_order, axis=0).transpose(0, 2, 1, 3)

    send_query = pack_out(query_rows)
    send_key = pack_out(key_rows)
    send_value = pack_out(value_rows)
    send_grad = pack_out(output_grad)
    moved = (
        lax.all_to_all(
            lax.all_to_all(send_query, "dp", split_axis=0, concat_axis=0, tiled=True),
            "seq",
            split_axis=1,
            concat_axis=1,
            tiled=True,
        ),
        lax.all_to_all(
            lax.all_to_all(send_key, "dp", split_axis=0, concat_axis=0, tiled=True),
            "seq",
            split_axis=1,
            concat_axis=1,
            tiled=True,
        ),
        lax.all_to_all(
            lax.all_to_all(send_value, "dp", split_axis=0, concat_axis=0, tiled=True),
            "seq",
            split_axis=1,
            concat_axis=1,
            tiled=True,
        ),
        lax.all_to_all(
            lax.all_to_all(send_grad, "dp", split_axis=0, concat_axis=0, tiled=True),
            "seq",
            split_axis=1,
            concat_axis=1,
            tiled=True,
        ),
    )
    slot_list = slot_sources[0]

    def unpack_in(tensor):
        ordered = jnp.take(tensor.reshape(source_count, block_rows, span_width), slot_list, axis=0)
        return ordered.reshape(seq_rows, heads_here, head_size)

    query_in = unpack_in(moved[0])
    key_in = unpack_in(moved[1])
    value_in = unpack_in(moved[2])
    grad_in = unpack_in(moved[3])
    clip_row = clip_index[0]
    query_wide = query_in.astype(jnp.float32)
    key_wide = key_in.astype(jnp.float32)
    query_inv, query_norm = norm_forward(query_wide, query_gain)
    key_inv, key_norm = norm_forward(key_wide, key_gain)
    score_scale = head_size ** (-0.5)
    block_len = min(512, seq_rows)
    block_total = seq_rows // block_len

    def visit(carry, block_id):
        key_acc, value_acc = carry
        start = block_id * block_len
        query_block = lax.dynamic_slice_in_dim(query_norm, start, block_len, 0)
        grad_block = lax.dynamic_slice_in_dim(grad_in, start, block_len, 0)
        clip_block = lax.dynamic_slice_in_dim(clip_row, start, block_len, 0)
        scores = (
            jnp.einsum("qhd,khd->hqk", query_block, key_norm, preferred_element_type=jnp.float32)
            * score_scale
        )
        same_clip = (clip_block[:, None] == clip_row[None, :])[None]
        masked = jnp.where(same_clip, scores, -1e30)
        row_top = jnp.max(masked, axis=-1, keepdims=True)
        weights = jnp.exp(masked - row_top)
        probs_full = weights / jnp.sum(weights, axis=-1, keepdims=True)
        probs_low = probs_full.astype(jnp.bfloat16)
        attended = jnp.einsum(
            "hqk,khd->qhd", probs_low, value_in, preferred_element_type=jnp.float32
        )
        value_acc = value_acc + jnp.einsum(
            "hqk,qhd->khd", probs_low, grad_block, preferred_element_type=jnp.float32
        )
        prob_grad = jnp.einsum(
            "qhd,khd->hqk", grad_block, value_in, preferred_element_type=jnp.float32
        )
        row_delta = jnp.sum(grad_block.astype(jnp.float32) * attended, axis=-1).T[:, :, None]
        score_grad = (probs_full * (prob_grad - row_delta) * score_scale).astype(jnp.bfloat16)
        query_grad_block = jnp.einsum(
            "hqk,khd->qhd", score_grad, key_norm, preferred_element_type=jnp.float32
        )
        key_acc = key_acc + jnp.einsum(
            "hqk,qhd->khd", score_grad, query_block, preferred_element_type=jnp.float32
        )
        return ((key_acc, value_acc), (attended.astype(jnp.bfloat16), query_grad_block))

    zero_state = jnp.zeros((seq_rows, heads_here, head_size), jnp.float32)
    (key_grad_norm, value_grad_wide), (attended_all, query_grad_norm) = lax.scan(
        visit, (zero_state, zero_state), jnp.arange(block_total)
    )
    query_grad_norm = query_grad_norm.reshape(seq_rows, heads_here, head_size)
    attended_all = attended_all.reshape(seq_rows, heads_here, head_size)
    query_grad, query_gain_grad = norm_backward(query_wide, query_inv, query_gain, query_grad_norm)
    key_grad, key_gain_grad = norm_backward(key_wide, key_inv, key_gain, key_grad_norm)
    value_grad = value_grad_wide.astype(jnp.bfloat16)
    source_ids = jnp.arange(source_count, dtype=jnp.int32)
    slot_of = jnp.sum(
        jnp.where(slot_list[None, :] == source_ids[:, None], source_ids[None, :], 0), axis=1
    )

    def pack_back(tensor):
        ordered = jnp.take(tensor.reshape(source_count, block_rows, span_width), slot_of, axis=0)
        return ordered.reshape(group_count, head_ways, block_rows, span_width)

    back_attended = pack_back(attended_all)
    back_query = pack_back(query_grad)
    back_key = pack_back(key_grad)
    back_value = pack_back(value_grad)
    homed = (
        lax.all_to_all(
            lax.all_to_all(back_attended, "dp", split_axis=0, concat_axis=0, tiled=True),
            "seq",
            split_axis=1,
            concat_axis=1,
            tiled=True,
        ),
        lax.all_to_all(
            lax.all_to_all(back_query, "dp", split_axis=0, concat_axis=0, tiled=True),
            "seq",
            split_axis=1,
            concat_axis=1,
            tiled=True,
        ),
        lax.all_to_all(
            lax.all_to_all(back_key, "dp", split_axis=0, concat_axis=0, tiled=True),
            "seq",
            split_axis=1,
            concat_axis=1,
            tiled=True,
        ),
        lax.all_to_all(
            lax.all_to_all(back_value, "dp", split_axis=0, concat_axis=0, tiled=True),
            "seq",
            split_axis=1,
            concat_axis=1,
            tiled=True,
        ),
    )

    def home_rows(tensor):
        return jnp.take(tensor, targets, axis=0).transpose(0, 2, 1, 3).reshape(tok_rows, full_width)

    gain_query, gain_key = lax.psum((query_gain_grad, key_gain_grad), ("dp", "seq"))
    factor = float(tok_rows * source_count * heads_total) ** (-0.5)
    gain_grads = jnp.stack([gain_query, gain_key]) * factor
    return (
        home_rows(homed[0]),
        home_rows(homed[1]),
        home_rows(homed[2]),
        home_rows(homed[3]),
        gain_grads,
    )


MESH = pl.DeviceIdType.MESH
NT = (((1,), (1,)), ((), ()))
TN = (((0,), (0,)), ((), ()))
NN = (((1,), (0,)), ((), ()))


def dot(a, b, dims):
    return lax.dot_general(a, b, dims, preferred_element_type=jnp.float32)


def fused_kernel(
    dims,
    dest_ref,
    slot_ref,
    clip_ref,
    qgain_ref,
    kgain_ref,
    q_ref,
    k_ref,
    v_ref,
    do_ref,
    att_ref,
    qg_ref,
    kg_ref,
    vg_ref,
    gain_ref,
    stage,
    recv,
    back,
    bias,
    gstage,
    grecv,
    order,
    send_sem,
    recv_sem,
    back_send_sem,
    back_recv_sem,
    gain_send_sem,
    gain_recv_sem,
    *homes,
):
    groups, ways, rows, chunks, width, heads, factor = dims
    n = groups * ways
    seq = n * rows
    span = chunks * width
    ins = (q_ref, k_ref, v_ref, do_ref)
    outs = (att_ref, qg_ref, kg_ref, vg_ref)
    me = lax.axis_index("dp") * ways + lax.axis_index("seq")
    stride = n // 2 + 1

    def peer(i):
        other = (me + i * stride) % n
        return other, (other // ways, other % ways)

    barrier = pltpu.get_barrier_semaphore()

    @pl.loop(1, n)
    def _(i):
        pl.semaphore_signal(barrier, inc=1, device_id=peer(i)[1], device_id_type=MESH)

    def pack(c):
        for t in range(4):
            for s in range(ways):
                part = ins[t][:, s * span + c * width : s * span + (c + 1) * width]
                part = dot(order[...], part, NN).astype(jnp.bfloat16)
                for g in range(groups):
                    stage[c, g * ways + s, t * rows : (t + 1) * rows, :] = part[
                        g * rows : (g + 1) * rows
                    ]

    def send_all(c):
        @pl.loop(1, n)
        def _(i):
            other, where = peer(i)
            pltpu.make_async_remote_copy(
                src_ref=stage.at[c, other],
                dst_ref=recv.at[c, me],
                send_sem=send_sem.at[c],
                recv_sem=recv_sem.at[c],
                device_id=where,
                device_id_type=MESH,
            ).start()

        recv[c, me] = stage[c, me]

    def return_all(c):
        @pl.loop(1, n)
        def _(i):
            other, where = peer(i)
            pltpu.make_async_remote_copy(
                src_ref=back.at[c, other],
                dst_ref=homes[c].at[me],
                send_sem=back_send_sem.at[c],
                recv_sem=back_recv_sem.at[c],
                device_id=where,
                device_id_type=MESH,
            ).start()

        homes[c][me] = back[c, me]

    def wait_bytes(ref, sem):
        pltpu.make_async_copy(ref, ref, sem).wait()

    row = lax.broadcasted_iota(jnp.int32, order.shape, 0)
    col = lax.broadcasted_iota(jnp.int32, order.shape, 1)
    joins = jnp.zeros(order.shape, jnp.int32)
    for j in range(groups):
        joins = joins + jnp.where(col // rows == j, dest_ref[0, j], 0)
    same = (row // rows == joins) & (row % rows == col % rows)
    order[...] = jnp.where(same, 1.0, 0.0).astype(jnp.bfloat16)

    pack(0)
    pl.semaphore_wait(barrier, n - 1)
    send_all(0)
    for c in range(1, chunks):
        pack(c)
        send_all(c)

    zeros = jnp.sum(jnp.where(clip_ref[...] == 0, 1.0, 0.0), axis=1, keepdims=True)
    lane = lax.broadcasted_iota(jnp.int32, (8, seq), 1)
    sub = lax.broadcasted_iota(jnp.int32, (seq, 128), 0)
    lane_src, sub_src = lane // rows, sub // rows
    lane_pos, sub_pos = lane % rows, sub % rows
    for t in range(n):
        src = slot_ref[0, t]
        lane_pos = lane_pos + jnp.where(lane_src == src, t * rows, 0)
        sub_pos = sub_pos + jnp.where(sub_src == src, t * rows, 0)
    lane_clip = jnp.where(lane_pos.astype(jnp.float32) >= zeros, 1.0, 0.0)[0:1]
    sub_clip = jnp.where(sub_pos.astype(jnp.float32) >= zeros, 1.0, 0.0)[:, 0:1]
    bias[...] = jnp.where(lane_clip == sub_clip, 0.0, -1e30)
    gstage[...] = jnp.zeros_like(gstage)

    hd = qgain_ref.shape[1]
    scale = hd ** (-0.5)
    gain_q = qgain_ref[...]
    gain_k = kgain_ref[...]

    def head_of(c, h):
        cols = pl.ds(pl.multiple_of(h * hd, hd), hd)

        def take(t):
            return recv[c, :, t * rows : (t + 1) * rows, cols].reshape(seq, hd)

        gq = take(0).astype(jnp.float32)
        gk = take(1).astype(jnp.float32)
        gv = take(2)
        gdo = take(3)
        rq = lax.rsqrt(jnp.mean(gq * gq, axis=-1, keepdims=True) + EPS)
        rk = lax.rsqrt(jnp.mean(gk * gk, axis=-1, keepdims=True) + EPS)
        qn = (gq * rq * gain_q).astype(jnp.bfloat16)
        kn = (gk * rk * gain_k).astype(jnp.bfloat16)
        masked = dot(qn, kn, NT) * scale + bias[...]
        weights = jnp.exp(masked - jnp.max(masked, axis=-1, keepdims=True))
        probs = weights / jnp.sum(weights, axis=-1, keepdims=True)
        low = probs.astype(jnp.bfloat16)
        att = dot(low, gv, NN)
        dv = dot(low, gdo, TN)
        dp = dot(gdo, gv, NT)
        delta = jnp.sum(gdo.astype(jnp.float32) * att, axis=-1, keepdims=True)
        ds = (probs * (dp - delta) * scale).astype(jnp.bfloat16)
        dqn = dot(ds, kn, NN)
        dkn = dot(ds, qn, TN)
        mq = jnp.mean(gain_q * dqn * gq, axis=-1, keepdims=True)
        mk = jnp.mean(gain_k * dkn * gk, axis=-1, keepdims=True)
        dq = rq * gain_q * dqn - gq * (rq * rq * rq) * mq
        dk = rk * gain_k * dkn - gk * (rk * rk * rk) * mk
        gstage[0:1, :] += jnp.sum(dqn * gq * rq, axis=0, keepdims=True)
        gstage[1:2, :] += jnp.sum(dkn * gk * rk, axis=0, keepdims=True)
        for t, res in enumerate((att, dq, dk, dv)):
            back[c, :, t * rows : (t + 1) * rows, cols] = res.astype(jnp.bfloat16).reshape(
                n, rows, hd
            )

    for c in range(chunks):
        wait_bytes(recv.at[c, pl.ds(0, n - 1)], recv_sem.at[c])

        @pl.loop(0, heads)
        def _(h):
            head_of(c, h)

        if c == chunks - 1:
            @pl.loop(1, n)
            def _(i):
                pltpu.make_async_remote_copy(
                    src_ref=gstage,
                    dst_ref=grecv.at[me],
                    send_sem=gain_send_sem,
                    recv_sem=gain_recv_sem,
                    device_id=peer(i)[1],
                    device_id_type=MESH,
                ).start()

            grecv[me] = gstage[...]
        return_all(c)

    for c in range(chunks):
        wait_bytes(homes[c].at[pl.ds(0, n - 1)], back_recv_sem.at[c])

        for s in range(ways):
            for t in range(4):
                part = jnp.concatenate(
                    [
                        homes[c][g * ways + s, t * rows : (t + 1) * rows, :]
                        for g in range(groups)
                    ],
                    axis=0,
                )
                outs[t][:, s * span + c * width : s * span + (c + 1) * width] = dot(
                    order[...], part, TN
                ).astype(jnp.bfloat16)

    wait_bytes(grecv.at[pl.ds(0, n - 1)], gain_recv_sem)
    gain_ref[...] = jnp.sum(grecv[...], axis=0)[0:2] * factor
    for c in range(chunks):
        wait_bytes(stage.at[c, pl.ds(0, n - 1)], send_sem.at[c])
        wait_bytes(back.at[c, pl.ds(0, n - 1)], back_send_sem.at[c])
    wait_bytes(grecv.at[pl.ds(0, n - 1)], gain_send_sem)


def shards_fused(
    query_rows,
    key_rows,
    value_rows,
    output_grad,
    query_gain,
    key_gain,
    dest_groups,
    slot_sources,
    clip_index,
):
    groups = lax.axis_size("dp")
    ways = lax.axis_size("seq")
    n = groups * ways
    tok, full = query_rows.shape
    hd = query_gain.shape[0]
    rows = tok // groups
    heads_here = full // hd // ways
    heads = 2 if heads_here % 2 == 0 else 1
    chunks = heads_here // heads
    width = heads * hd
    seq = tok * ways
    factor = float(tok * n * (full // hd)) ** (-0.5)
    dims = (groups, ways, rows, chunks, width, heads, factor)
    vmem = pl.BlockSpec(memory_space=pltpu.VMEM)
    smem = pl.BlockSpec(memory_space=pltpu.SMEM)
    slab = (n, 4 * rows, width)
    bf = jnp.bfloat16
    out = jax.ShapeDtypeStruct((tok, full), bf)
    dma = pltpu.SemaphoreType.DMA
    return pl.pallas_call(
        functools.partial(fused_kernel, dims),
        out_shape=(out, out, out, out, jax.ShapeDtypeStruct((2, hd), jnp.float32)),
        in_specs=[smem, smem] + [vmem] * 7,
        out_specs=(vmem,) * 5,
        scratch_shapes=[
            pltpu.VMEM((chunks,) + slab, bf),
            pltpu.VMEM((chunks,) + slab, bf),
            pltpu.VMEM((chunks,) + slab, bf),
            pltpu.VMEM((seq, seq), jnp.float32),
            pltpu.VMEM((8, hd), jnp.float32),
            pltpu.VMEM((n, 8, hd), jnp.float32),
            pltpu.VMEM((tok, tok), bf),
            dma((chunks,)),
            dma((chunks,)),
            dma((chunks,)),
            dma((chunks,)),
            dma,
            dma,
        ]
        + [pltpu.VMEM(slab, bf)] * chunks,
        compiler_params=pltpu.CompilerParams(
            collective_id=0, has_side_effects=True, vmem_limit_bytes=48 * 2**20
        ),
    )(
        dest_groups,
        slot_sources,
        clip_index,
        query_gain.reshape(1, hd),
        key_gain.reshape(1, hd),
        query_rows,
        key_rows,
        value_rows,
        output_grad,
    )


def shards(query_rows, *rest):
    if (query_rows.shape[0] // lax.axis_size("dp")) % 16 == 0:
        return shards_fused(query_rows, *rest)
    return shards_plain(query_rows, *rest)


def solution(mesh):
    return jax.shard_map(
        shards,
        mesh=mesh,
        in_specs=(
            P(("dp", "seq"), None),
            P(("dp", "seq"), None),
            P(("dp", "seq"), None),
            P(("dp", "seq"), None),
            P(),
            P(),
            P(("dp", "seq"), None),
            P("dp", None),
            P("dp", None),
        ),
        out_specs=(
            P(("dp", "seq"), None),
            P(("dp", "seq"), None),
            P(("dp", "seq"), None),
            P(("dp", "seq"), None),
            P(),
        ),
        check_vma=False,
    )
```

```python
import functools

import jax
import jax.numpy as jnp
from jax import lax
from jax.experimental import pallas as pl
from jax.experimental.pallas import tpu as pltpu
from jax.sharding import PartitionSpec as P

EPS = 1e-06


def norm_forward(tensor, gain_vec):
    inverse = lax.rsqrt(jnp.mean(tensor * tensor, axis=-1, keepdims=True) + EPS)
    return (inverse, (tensor * inverse * gain_vec).astype(jnp.bfloat16))


def norm_backward(tensor, inverse, gain_vec, upstream):
    inner_mean = jnp.mean(gain_vec * upstream * tensor, axis=-1, keepdims=True)
    grad_input = inverse * gain_vec * upstream - tensor * inverse**3 * inner_mean
    grad_gain = jnp.sum(upstream * tensor * inverse, axis=(0, 1))
    return (grad_input.astype(jnp.bfloat16), grad_gain)


def shards_plain(
    query_rows,
    key_rows,
    value_rows,
    output_grad,
    query_gain,
    key_gain,
    dest_groups,
    slot_sources,
    clip_index,
):
    group_count = lax.axis_size("dp")
    head_ways = lax.axis_size("seq")
    tok_rows, full_width = query_rows.shape
    head_size = query_gain.shape[0]
    heads_total = full_width // head_size
    heads_here = heads_total // head_ways
    span_width = heads_here * head_size
    block_rows = tok_rows // group_count
    source_count = group_count * head_ways
    seq_rows = tok_rows * head_ways
    targets = dest_groups[0]
    group_ids = jnp.arange(group_count, dtype=jnp.int32)
    block_order = jnp.sum(
        jnp.where(targets[None, :] == group_ids[:, None], group_ids[None, :], 0), axis=1
    )

    def pack_out(tensor):
        blocks = tensor.reshape(group_count, block_rows, head_ways, span_width)
        return jnp.take(blocks, block_order, axis=0).transpose(0, 2, 1, 3)

    send_query = pack_out(query_rows)
    send_key = pack_out(key_rows)
    send_value = pack_out(value_rows)
    send_grad = pack_out(output_grad)
    moved = (
        lax.all_to_all(
            lax.all_to_all(send_query, "dp", split_axis=0, concat_axis=0, tiled=True),
            "seq",
            split_axis=1,
            concat_axis=1,
            tiled=True,
        ),
        lax.all_to_all(
            lax.all_to_all(send_key, "dp", split_axis=0, concat_axis=0, tiled=True),
            "seq",
            split_axis=1,
            concat_axis=1,
            tiled=True,
        ),
        lax.all_to_all(
            lax.all_to_all(send_value, "dp", split_axis=0, concat_axis=0, tiled=True),
            "seq",
            split_axis=1,
            concat_axis=1,
            tiled=True,
        ),
        lax.all_to_all(
            lax.all_to_all(send_grad, "dp", split_axis=0, concat_axis=0, tiled=True),
            "seq",
            split_axis=1,
            concat_axis=1,
            tiled=True,
        ),
    )
    slot_list = slot_sources[0]

    def unpack_in(tensor):
        ordered = jnp.take(tensor.reshape(source_count, block_rows, span_width), slot_list, axis=0)
        return ordered.reshape(seq_rows, heads_here, head_size)

    query_in = unpack_in(moved[0])
    key_in = unpack_in(moved[1])
    value_in = unpack_in(moved[2])
    grad_in = unpack_in(moved[3])
    clip_row = clip_index[0]
    query_wide = query_in.astype(jnp.float32)
    key_wide = key_in.astype(jnp.float32)
    query_inv, query_norm = norm_forward(query_wide, query_gain)
    key_inv, key_norm = norm_forward(key_wide, key_gain)
    score_scale = head_size ** (-0.5)
    block_len = min(512, seq_rows)
    block_total = seq_rows // block_len

    def visit(carry, block_id):
        key_acc, value_acc = carry
        start = block_id * block_len
        query_block = lax.dynamic_slice_in_dim(query_norm, start, block_len, 0)
        grad_block = lax.dynamic_slice_in_dim(grad_in, start, block_len, 0)
        clip_block = lax.dynamic_slice_in_dim(clip_row, start, block_len, 0)
        scores = (
            jnp.einsum("qhd,khd->hqk", query_block, key_norm, preferred_element_type=jnp.float32)
            * score_scale
        )
        same_clip = (clip_block[:, None] == clip_row[None, :])[None]
        masked = jnp.where(same_clip, scores, -1e30)
        row_top = jnp.max(masked, axis=-1, keepdims=True)
        weights = jnp.exp(masked - row_top)
        probs_full = weights / jnp.sum(weights, axis=-1, keepdims=True)
        probs_low = probs_full.astype(jnp.bfloat16)
        attended = jnp.einsum(
            "hqk,khd->qhd", probs_low, value_in, preferred_element_type=jnp.float32
        )
        value_acc = value_acc + jnp.einsum(
            "hqk,qhd->khd", probs_low, grad_block, preferred_element_type=jnp.float32
        )
        prob_grad = jnp.einsum(
            "qhd,khd->hqk", grad_block, value_in, preferred_element_type=jnp.float32
        )
        row_delta = jnp.sum(grad_block.astype(jnp.float32) * attended, axis=-1).T[:, :, None]
        score_grad = (probs_full * (prob_grad - row_delta) * score_scale).astype(jnp.bfloat16)
        query_grad_block = jnp.einsum(
            "hqk,khd->qhd", score_grad, key_norm, preferred_element_type=jnp.float32
        )
        key_acc = key_acc + jnp.einsum(
            "hqk,qhd->khd", score_grad, query_block, preferred_element_type=jnp.float32
        )
        return ((key_acc, value_acc), (attended.astype(jnp.bfloat16), query_grad_block))

    zero_state = jnp.zeros((seq_rows, heads_here, head_size), jnp.float32)
    (key_grad_norm, value_grad_wide), (attended_all, query_grad_norm) = lax.scan(
        visit, (zero_state, zero_state), jnp.arange(block_total)
    )
    query_grad_norm = query_grad_norm.reshape(seq_rows, heads_here, head_size)
    attended_all = attended_all.reshape(seq_rows, heads_here, head_size)
    query_grad, query_gain_grad = norm_backward(query_wide, query_inv, query_gain, query_grad_norm)
    key_grad, key_gain_grad = norm_backward(key_wide, key_inv, key_gain, key_grad_norm)
    value_grad = value_grad_wide.astype(jnp.bfloat16)
    source_ids = jnp.arange(source_count, dtype=jnp.int32)
    slot_of = jnp.sum(
        jnp.where(slot_list[None, :] == source_ids[:, None], source_ids[None, :], 0), axis=1
    )

    def pack_back(tensor):
        ordered = jnp.take(tensor.reshape(source_count, block_rows, span_width), slot_of, axis=0)
        return ordered.reshape(group_count, head_ways, block_rows, span_width)

    back_attended = pack_back(attended_all)
    back_query = pack_back(query_grad)
    back_key = pack_back(key_grad)
    back_value = pack_back(value_grad)
    homed = (
        lax.all_to_all(
            lax.all_to_all(back_attended, "dp", split_axis=0, concat_axis=0, tiled=True),
            "seq",
            split_axis=1,
            concat_axis=1,
            tiled=True,
        ),
        lax.all_to_all(
            lax.all_to_all(back_query, "dp", split_axis=0, concat_axis=0, tiled=True),
            "seq",
            split_axis=1,
            concat_axis=1,
            tiled=True,
        ),
        lax.all_to_all(
            lax.all_to_all(back_key, "dp", split_axis=0, concat_axis=0, tiled=True),
            "seq",
            split_axis=1,
            concat_axis=1,
            tiled=True,
        ),
        lax.all_to_all(
            lax.all_to_all(back_value, "dp", split_axis=0, concat_axis=0, tiled=True),
            "seq",
            split_axis=1,
            concat_axis=1,
            tiled=True,
        ),
    )

    def home_rows(tensor):
        return jnp.take(tensor, targets, axis=0).transpose(0, 2, 1, 3).reshape(tok_rows, full_width)

    gain_query, gain_key = lax.psum((query_gain_grad, key_gain_grad), ("dp", "seq"))
    factor = float(tok_rows * source_count * heads_total) ** (-0.5)
    gain_grads = jnp.stack([gain_query, gain_key]) * factor
    return (
        home_rows(homed[0]),
        home_rows(homed[1]),
        home_rows(homed[2]),
        home_rows(homed[3]),
        gain_grads,
    )


MESH = pl.DeviceIdType.MESH
NT = (((1,), (1,)), ((), ()))
TN = (((0,), (0,)), ((), ()))
NN = (((1,), (0,)), ((), ()))


def dot(a, b, dims):
    return lax.dot_general(a, b, dims, preferred_element_type=jnp.float32)


def block_order(dest_ref, groups, rows):
    shape = (groups * rows, groups * rows)
    row = lax.broadcasted_iota(jnp.int32, shape, 0)
    col = lax.broadcasted_iota(jnp.int32, shape, 1)
    joins = jnp.zeros(shape, jnp.int32)
    for j in range(groups):
        joins = joins + jnp.where(col // rows == j, dest_ref[0, j], 0)
    same = (row // rows == joins) & (row % rows == col % rows)
    return jnp.where(same, 1.0, 0.0).astype(jnp.bfloat16)


def home_kernel(dims, factor, dest_ref, grecv, *refs):
    groups, ways, rows, chunks, width, heads = dims
    span = chunks * width
    homes, outs = refs[:chunks], refs[chunks : chunks + 4]
    gain_ref, held, sem, got, got_sem = refs[chunks + 4 :]
    joins = [dest_ref[0, j] for j in range(groups)]
    loads = [pltpu.make_async_copy(homes[c], got.at[c], got_sem.at[c]) for c in range(chunks)]
    for load in loads:
        load.start()
    for load in loads:
        load.wait()
    copies = []
    for t in range(4):
        for c in range(chunks):
            for s in range(ways):
                for j in range(groups):
                    held[
                        t,
                        j * rows : (j + 1) * rows,
                        s * span + c * width : s * span + (c + 1) * width,
                    ] = got[c, joins[j] * ways + s, t * rows : (t + 1) * rows, :]
        copies.append(pltpu.make_async_copy(held.at[t], outs[t], sem.at[t]))
        copies[t].start()
    hd = gain_ref.shape[1]
    total = jnp.sum(grecv[...], axis=0) * factor
    gain_ref[0:1, :] = total[:, 0:hd]
    gain_ref[1:2, :] = total[:, hd : 2 * hd]
    for copy in copies:
        copy.wait()


def fused_kernel(
    dims,
    dest_ref,
    slot_ref,
    clip_ref,
    qgain_ref,
    kgain_ref,
    q_ref,
    k_ref,
    v_ref,
    do_ref,
    grecv,
    *rest,
):
    groups, ways, rows, chunks, width, heads = dims
    homes = rest[:chunks]
    stage, recv, back, bias, gstage, order, rows_in = rest[chunks : chunks + 7]
    in_sem, send_sem, recv_sem, back_send_sem, back_recv_sem = rest[chunks + 7 : chunks + 12]
    own_sem, gain_send_sem, gain_recv_sem = rest[chunks + 12 :]
    n = groups * ways
    seq = n * rows
    span = chunks * width
    ins = (q_ref, k_ref, v_ref, do_ref)
    me = lax.axis_index("dp") * ways + lax.axis_index("seq")
    stride = n // 2 + 1

    def peer(i):
        other = (me + i * stride) % n
        return other, (other // ways, other % ways)

    loads = [pltpu.make_async_copy(ins[t], rows_in.at[t], in_sem.at[t]) for t in range(4)]
    for load in loads:
        load.start()
    barrier = pltpu.get_barrier_semaphore()

    @pl.loop(1, n)
    def _(i):
        pl.semaphore_signal(barrier, inc=1, device_id=peer(i)[1], device_id_type=MESH)

    def pack(c):
        for t in range(4):
            for s in range(ways):
                part = rows_in[t, :, s * span + c * width : s * span + (c + 1) * width]
                part = dot(order[...], part, NN).astype(jnp.bfloat16)
                for g in range(groups):
                    stage[c, g * ways + s, t * rows : (t + 1) * rows, :] = part[
                        g * rows : (g + 1) * rows
                    ]

    def send_all(c):
        @pl.loop(1, n)
        def _(i):
            other, where = peer(i)
            pltpu.make_async_remote_copy(
                src_ref=stage.at[c, other],
                dst_ref=recv.at[c, me],
                send_sem=send_sem.at[c],
                recv_sem=recv_sem.at[c],
                device_id=where,
                device_id_type=MESH,
            ).start()

        recv[c, me] = stage[c, me]

    def return_all(c):
        @pl.loop(1, n)
        def _(i):
            other, where = peer(i)
            pltpu.make_async_remote_copy(
                src_ref=back.at[c, other],
                dst_ref=homes[c].at[me],
                send_sem=back_send_sem.at[c],
                recv_sem=back_recv_sem.at[c],
                device_id=where,
                device_id_type=MESH,
            ).start()

        pltpu.make_async_copy(back.at[c, me], homes[c].at[me], own_sem.at[c]).start()

    def wait_bytes(ref, sem):
        pltpu.make_async_copy(ref, ref, sem).wait()

    order[...] = block_order(dest_ref, groups, rows)
    for load in loads:
        load.wait()

    pack(0)
    pl.semaphore_wait(barrier, n - 1)
    send_all(0)
    for c in range(1, chunks):
        pack(c)
        send_all(c)

    zeros = jnp.sum(jnp.where(clip_ref[...] == 0, 1.0, 0.0), axis=1, keepdims=True)
    lane = lax.broadcasted_iota(jnp.int32, (8, seq), 1)
    sub = lax.broadcasted_iota(jnp.int32, (seq, 128), 0)
    lane_src, sub_src = lane // rows, sub // rows
    lane_pos, sub_pos = lane % rows, sub % rows
    for t in range(n):
        src = slot_ref[0, t]
        lane_pos = lane_pos + jnp.where(lane_src == src, t * rows, 0)
        sub_pos = sub_pos + jnp.where(sub_src == src, t * rows, 0)
    lane_clip = jnp.where(lane_pos.astype(jnp.float32) >= zeros, 1.0, 0.0)[0:1]
    sub_clip = jnp.where(sub_pos.astype(jnp.float32) >= zeros, 1.0, 0.0)[:, 0:1]
    bias[...] = jnp.where(lane_clip == sub_clip, 0.0, -1e30)
    gstage[...] = jnp.zeros_like(gstage)

    hd = qgain_ref.shape[1]
    scale = hd ** (-0.5)
    gain_q = qgain_ref[...]
    gain_k = kgain_ref[...]

    def head_of(c, h):
        cols = pl.ds(pl.multiple_of(h * hd, hd), hd)

        def take(t):
            return recv[c, :, t * rows : (t + 1) * rows, cols].reshape(seq, hd)

        gq = take(0).astype(jnp.float32)
        gk = take(1).astype(jnp.float32)
        gv = take(2)
        gdo = take(3)
        rq = lax.rsqrt(jnp.mean(gq * gq, axis=-1, keepdims=True) + EPS)
        rk = lax.rsqrt(jnp.mean(gk * gk, axis=-1, keepdims=True) + EPS)
        qn = (gq * rq * gain_q).astype(jnp.bfloat16)
        kn = (gk * rk * gain_k).astype(jnp.bfloat16)
        masked = dot(qn, kn, NT) * scale + bias[...]
        weights = jnp.exp(masked - jnp.max(masked, axis=-1, keepdims=True))
        probs = weights / jnp.sum(weights, axis=-1, keepdims=True)
        low = probs.astype(jnp.bfloat16)
        att = dot(low, gv, NN)
        dv = dot(low, gdo, TN)
        dp = dot(gdo, gv, NT)
        delta = jnp.sum(gdo.astype(jnp.float32) * att, axis=-1, keepdims=True)
        ds = (probs * (dp - delta) * scale).astype(jnp.bfloat16)
        dqn = dot(ds, kn, NN)
        dkn = dot(ds, qn, TN)
        mq = jnp.mean(gain_q * dqn * gq, axis=-1, keepdims=True)
        mk = jnp.mean(gain_k * dkn * gk, axis=-1, keepdims=True)
        dq = rq * gain_q * dqn - gq * (rq * rq * rq) * mq
        dk = rk * gain_k * dkn - gk * (rk * rk * rk) * mk
        gstage[:, 0:hd] += jnp.sum(dqn * gq * rq, axis=0, keepdims=True)
        gstage[:, hd : 2 * hd] += jnp.sum(dkn * gk * rk, axis=0, keepdims=True)
        for t, res in enumerate((att, dq, dk, dv)):
            back[c, :, t * rows : (t + 1) * rows, cols] = res.astype(jnp.bfloat16).reshape(
                n, rows, hd
            )

    for c in range(chunks):
        wait_bytes(recv.at[c, pl.ds(0, n - 1)], recv_sem.at[c])

        @pl.loop(0, heads)
        def _(h):
            head_of(c, h)

        if c == chunks - 1:
            @pl.loop(1, n)
            def _(i):
                pltpu.make_async_remote_copy(
                    src_ref=gstage,
                    dst_ref=grecv.at[me],
                    send_sem=gain_send_sem,
                    recv_sem=gain_recv_sem,
                    device_id=peer(i)[1],
                    device_id_type=MESH,
                ).start()

            grecv[me] = gstage[...]
        return_all(c)

    for c in range(chunks):
        wait_bytes(homes[c].at[pl.ds(0, n - 1)], back_recv_sem.at[c])
    wait_bytes(grecv.at[pl.ds(0, n - 1)], gain_recv_sem)
    for c in range(chunks):
        wait_bytes(stage.at[c, pl.ds(0, n - 1)], send_sem.at[c])
        wait_bytes(back.at[c, pl.ds(0, n - 1)], back_send_sem.at[c])
        pltpu.make_async_copy(back.at[c, me], homes[c].at[me], own_sem.at[c]).wait()
    wait_bytes(grecv.at[pl.ds(0, n - 1)], gain_send_sem)


def shards_fused(
    query_rows,
    key_rows,
    value_rows,
    output_grad,
    query_gain,
    key_gain,
    dest_groups,
    slot_sources,
    clip_index,
):
    groups = lax.axis_size("dp")
    ways = lax.axis_size("seq")
    n = groups * ways
    tok, full = query_rows.shape
    hd = query_gain.shape[0]
    rows = tok // groups
    heads_here = full // hd // ways
    heads = 2 if heads_here % 2 == 0 else 1
    chunks = heads_here // heads
    width = heads * hd
    seq = tok * ways
    factor = float(tok * n * (full // hd)) ** (-0.5)
    dims = (groups, ways, rows, chunks, width, heads)
    vmem = pl.BlockSpec(memory_space=pltpu.VMEM)
    smem = pl.BlockSpec(memory_space=pltpu.SMEM)
    slab = (n, 4 * rows, width)
    bf = jnp.bfloat16
    out = jax.ShapeDtypeStruct((tok, full), bf)
    dma = pltpu.SemaphoreType.DMA
    hbm = pl.BlockSpec(memory_space=pl.ANY)
    landed = pl.pallas_call(
        functools.partial(fused_kernel, dims),
        out_shape=[jax.ShapeDtypeStruct((n, 1, 2 * hd), jnp.float32)]
        + [jax.ShapeDtypeStruct(slab, bf)] * chunks,
        in_specs=[smem, smem] + [vmem] * 3 + [hbm] * 4,
        out_specs=[vmem] + [hbm] * chunks,
        scratch_shapes=[
            pltpu.VMEM((chunks,) + slab, bf),
            pltpu.VMEM((chunks,) + slab, bf),
            pltpu.VMEM((chunks,) + slab, bf),
            pltpu.VMEM((seq, seq), jnp.float32),
            pltpu.VMEM((1, 2 * hd), jnp.float32),
            pltpu.VMEM((tok, tok), bf),
            pltpu.VMEM((4, tok, full), bf),
            dma((4,)),
            dma((chunks,)),
            dma((chunks,)),
            dma((chunks,)),
            dma((chunks,)),
            dma((chunks,)),
            dma,
            dma,
        ],
        compiler_params=pltpu.CompilerParams(
            collective_id=0, has_side_effects=True, vmem_limit_bytes=60 * 2**20
        ),
    )(
        dest_groups,
        slot_sources,
        clip_index,
        query_gain.reshape(1, hd),
        key_gain.reshape(1, hd),
        query_rows,
        key_rows,
        value_rows,
        output_grad,
    )
    return pl.pallas_call(
        functools.partial(home_kernel, dims, factor),
        out_shape=(out, out, out, out, jax.ShapeDtypeStruct((2, hd), jnp.float32)),
        in_specs=[smem, vmem] + [hbm] * chunks,
        out_specs=(hbm,) * 4 + (vmem,),
        scratch_shapes=[
            pltpu.VMEM((4, tok, full), bf),
            dma((4,)),
            pltpu.VMEM((chunks,) + slab, bf),
            dma((chunks,)),
        ],
        compiler_params=pltpu.CompilerParams(vmem_limit_bytes=60 * 2**20),
    )(dest_groups, *landed)


def shards(query_rows, *rest):
    if (query_rows.shape[0] // lax.axis_size("dp")) % 16 == 0:
        return shards_fused(query_rows, *rest)
    return shards_plain(query_rows, *rest)


def solution(mesh):
    return jax.shard_map(
        shards,
        mesh=mesh,
        in_specs=(
            P(("dp", "seq"), None),
            P(("dp", "seq"), None),
            P(("dp", "seq"), None),
            P(("dp", "seq"), None),
            P(),
            P(),
            P(("dp", "seq"), None),
            P("dp", None),
            P("dp", None),
        ),
        out_specs=(
            P(("dp", "seq"), None),
            P(("dp", "seq"), None),
            P(("dp", "seq"), None),
            P(("dp", "seq"), None),
            P(),
        ),
        check_vma=False,
    )
```

```python
import functools

import jax
import jax.numpy as jnp
from jax import lax
from jax.experimental import pallas as pl
from jax.experimental.pallas import tpu as pltpu
from jax.sharding import PartitionSpec as P

EPS = 1e-06


def norm_forward(tensor, gain_vec):
    inverse = lax.rsqrt(jnp.mean(tensor * tensor, axis=-1, keepdims=True) + EPS)
    return (inverse, (tensor * inverse * gain_vec).astype(jnp.bfloat16))


def norm_backward(tensor, inverse, gain_vec, upstream):
    inner_mean = jnp.mean(gain_vec * upstream * tensor, axis=-1, keepdims=True)
    grad_input = inverse * gain_vec * upstream - tensor * inverse**3 * inner_mean
    grad_gain = jnp.sum(upstream * tensor * inverse, axis=(0, 1))
    return (grad_input.astype(jnp.bfloat16), grad_gain)


def shards_plain(
    query_rows,
    key_rows,
    value_rows,
    output_grad,
    query_gain,
    key_gain,
    dest_groups,
    slot_sources,
    clip_index,
):
    group_count = lax.axis_size("dp")
    head_ways = lax.axis_size("seq")
    tok_rows, full_width = query_rows.shape
    head_size = query_gain.shape[0]
    heads_total = full_width // head_size
    heads_here = heads_total // head_ways
    span_width = heads_here * head_size
    block_rows = tok_rows // group_count
    source_count = group_count * head_ways
    seq_rows = tok_rows * head_ways
    targets = dest_groups[0]
    group_ids = jnp.arange(group_count, dtype=jnp.int32)
    block_order = jnp.sum(
        jnp.where(targets[None, :] == group_ids[:, None], group_ids[None, :], 0), axis=1
    )

    def pack_out(tensor):
        blocks = tensor.reshape(group_count, block_rows, head_ways, span_width)
        return jnp.take(blocks, block_order, axis=0).transpose(0, 2, 1, 3)

    send_query = pack_out(query_rows)
    send_key = pack_out(key_rows)
    send_value = pack_out(value_rows)
    send_grad = pack_out(output_grad)
    moved = (
        lax.all_to_all(
            lax.all_to_all(send_query, "dp", split_axis=0, concat_axis=0, tiled=True),
            "seq",
            split_axis=1,
            concat_axis=1,
            tiled=True,
        ),
        lax.all_to_all(
            lax.all_to_all(send_key, "dp", split_axis=0, concat_axis=0, tiled=True),
            "seq",
            split_axis=1,
            concat_axis=1,
            tiled=True,
        ),
        lax.all_to_all(
            lax.all_to_all(send_value, "dp", split_axis=0, concat_axis=0, tiled=True),
            "seq",
            split_axis=1,
            concat_axis=1,
            tiled=True,
        ),
        lax.all_to_all(
            lax.all_to_all(send_grad, "dp", split_axis=0, concat_axis=0, tiled=True),
            "seq",
            split_axis=1,
            concat_axis=1,
            tiled=True,
        ),
    )
    slot_list = slot_sources[0]

    def unpack_in(tensor):
        ordered = jnp.take(tensor.reshape(source_count, block_rows, span_width), slot_list, axis=0)
        return ordered.reshape(seq_rows, heads_here, head_size)

    query_in = unpack_in(moved[0])
    key_in = unpack_in(moved[1])
    value_in = unpack_in(moved[2])
    grad_in = unpack_in(moved[3])
    clip_row = clip_index[0]
    query_wide = query_in.astype(jnp.float32)
    key_wide = key_in.astype(jnp.float32)
    query_inv, query_norm = norm_forward(query_wide, query_gain)
    key_inv, key_norm = norm_forward(key_wide, key_gain)
    score_scale = head_size ** (-0.5)
    block_len = min(512, seq_rows)
    block_total = seq_rows // block_len

    def visit(carry, block_id):
        key_acc, value_acc = carry
        start = block_id * block_len
        query_block = lax.dynamic_slice_in_dim(query_norm, start, block_len, 0)
        grad_block = lax.dynamic_slice_in_dim(grad_in, start, block_len, 0)
        clip_block = lax.dynamic_slice_in_dim(clip_row, start, block_len, 0)
        scores = (
            jnp.einsum("qhd,khd->hqk", query_block, key_norm, preferred_element_type=jnp.float32)
            * score_scale
        )
        same_clip = (clip_block[:, None] == clip_row[None, :])[None]
        masked = jnp.where(same_clip, scores, -1e30)
        row_top = jnp.max(masked, axis=-1, keepdims=True)
        weights = jnp.exp(masked - row_top)
        probs_full = weights / jnp.sum(weights, axis=-1, keepdims=True)
        probs_low = probs_full.astype(jnp.bfloat16)
        attended = jnp.einsum(
            "hqk,khd->qhd", probs_low, value_in, preferred_element_type=jnp.float32
        )
        value_acc = value_acc + jnp.einsum(
            "hqk,qhd->khd", probs_low, grad_block, preferred_element_type=jnp.float32
        )
        prob_grad = jnp.einsum(
            "qhd,khd->hqk", grad_block, value_in, preferred_element_type=jnp.float32
        )
        row_delta = jnp.sum(grad_block.astype(jnp.float32) * attended, axis=-1).T[:, :, None]
        score_grad = (probs_full * (prob_grad - row_delta) * score_scale).astype(jnp.bfloat16)
        query_grad_block = jnp.einsum(
            "hqk,khd->qhd", score_grad, key_norm, preferred_element_type=jnp.float32
        )
        key_acc = key_acc + jnp.einsum(
            "hqk,qhd->khd", score_grad, query_block, preferred_element_type=jnp.float32
        )
        return ((key_acc, value_acc), (attended.astype(jnp.bfloat16), query_grad_block))

    zero_state = jnp.zeros((seq_rows, heads_here, head_size), jnp.float32)
    (key_grad_norm, value_grad_wide), (attended_all, query_grad_norm) = lax.scan(
        visit, (zero_state, zero_state), jnp.arange(block_total)
    )
    query_grad_norm = query_grad_norm.reshape(seq_rows, heads_here, head_size)
    attended_all = attended_all.reshape(seq_rows, heads_here, head_size)
    query_grad, query_gain_grad = norm_backward(query_wide, query_inv, query_gain, query_grad_norm)
    key_grad, key_gain_grad = norm_backward(key_wide, key_inv, key_gain, key_grad_norm)
    value_grad = value_grad_wide.astype(jnp.bfloat16)
    source_ids = jnp.arange(source_count, dtype=jnp.int32)
    slot_of = jnp.sum(
        jnp.where(slot_list[None, :] == source_ids[:, None], source_ids[None, :], 0), axis=1
    )

    def pack_back(tensor):
        ordered = jnp.take(tensor.reshape(source_count, block_rows, span_width), slot_of, axis=0)
        return ordered.reshape(group_count, head_ways, block_rows, span_width)

    back_attended = pack_back(attended_all)
    back_query = pack_back(query_grad)
    back_key = pack_back(key_grad)
    back_value = pack_back(value_grad)
    homed = (
        lax.all_to_all(
            lax.all_to_all(back_attended, "dp", split_axis=0, concat_axis=0, tiled=True),
            "seq",
            split_axis=1,
            concat_axis=1,
            tiled=True,
        ),
        lax.all_to_all(
            lax.all_to_all(back_query, "dp", split_axis=0, concat_axis=0, tiled=True),
            "seq",
            split_axis=1,
            concat_axis=1,
            tiled=True,
        ),
        lax.all_to_all(
            lax.all_to_all(back_key, "dp", split_axis=0, concat_axis=0, tiled=True),
            "seq",
            split_axis=1,
            concat_axis=1,
            tiled=True,
        ),
        lax.all_to_all(
            lax.all_to_all(back_value, "dp", split_axis=0, concat_axis=0, tiled=True),
            "seq",
            split_axis=1,
            concat_axis=1,
            tiled=True,
        ),
    )

    def home_rows(tensor):
        return jnp.take(tensor, targets, axis=0).transpose(0, 2, 1, 3).reshape(tok_rows, full_width)

    gain_query, gain_key = lax.psum((query_gain_grad, key_gain_grad), ("dp", "seq"))
    factor = float(tok_rows * source_count * heads_total) ** (-0.5)
    gain_grads = jnp.stack([gain_query, gain_key]) * factor
    return (
        home_rows(homed[0]),
        home_rows(homed[1]),
        home_rows(homed[2]),
        home_rows(homed[3]),
        gain_grads,
    )


MESH = pl.DeviceIdType.MESH
NT = (((1,), (1,)), ((), ()))
TN = (((0,), (0,)), ((), ()))
NN = (((1,), (0,)), ((), ()))


def dot(a, b, dims):
    return lax.dot_general(a, b, dims, preferred_element_type=jnp.float32)


def block_order(dest_ref, groups, rows):
    shape = (groups * rows, groups * rows)
    row = lax.broadcasted_iota(jnp.int32, shape, 0)
    col = lax.broadcasted_iota(jnp.int32, shape, 1)
    joins = jnp.zeros(shape, jnp.int32)
    for j in range(groups):
        joins = joins + jnp.where(col // rows == j, dest_ref[0, j], 0)
    same = (row // rows == joins) & (row % rows == col % rows)
    return jnp.where(same, 1.0, 0.0).astype(jnp.bfloat16)


def home_kernel(dims, factor, dest_ref, grecv, *refs):
    groups, ways, rows, chunks, width, heads = dims
    span = chunks * width
    homes, outs = refs[:chunks], refs[chunks : chunks + 4]
    gain_ref, held, sem, got, got_sem = refs[chunks + 4 :]
    joins = [dest_ref[0, j] for j in range(groups)]
    loads = [pltpu.make_async_copy(homes[c], got.at[c], got_sem.at[c]) for c in range(chunks)]
    for load in loads:
        load.start()
    for load in loads:
        load.wait()
    copies = []
    for t in range(4):
        for c in range(chunks):
            for s in range(ways):
                for j in range(groups):
                    held[
                        t,
                        j * rows : (j + 1) * rows,
                        s * span + c * width : s * span + (c + 1) * width,
                    ] = got[c, joins[j] * ways + s, t * rows : (t + 1) * rows, :]
        copies.append(pltpu.make_async_copy(held.at[t], outs[t], sem.at[t]))
        copies[t].start()
    hd = gain_ref.shape[1]
    total = jnp.sum(grecv[...], axis=0) * factor
    gain_ref[0:1, :] = total[:, 0:hd]
    gain_ref[1:2, :] = total[:, hd : 2 * hd]
    for copy in copies:
        copy.wait()


def fused_kernel(
    dims,
    dest_ref,
    slot_ref,
    clip_ref,
    qgain_ref,
    kgain_ref,
    q_ref,
    k_ref,
    v_ref,
    do_ref,
    grecv,
    *rest,
):
    groups, ways, rows, chunks, width, heads = dims
    homes = rest[:chunks]
    stage, recv, back, bias, gstage, order, rows_in = rest[chunks : chunks + 7]
    in_sem, send_sem, recv_sem, back_send_sem, back_recv_sem = rest[chunks + 7 : chunks + 12]
    own_sem, gain_send_sem, gain_recv_sem = rest[chunks + 12 :]
    n = groups * ways
    seq = n * rows
    span = chunks * width
    ins = (q_ref, k_ref, v_ref, do_ref)
    me = lax.axis_index("dp") * ways + lax.axis_index("seq")
    stride = n // 2 + 1

    def peer(i):
        other = (me + i * stride) % n
        return other, (other // ways, other % ways)


    def load(c, t, s):
        cols = pl.ds(s * span + c * width, width)
        return pltpu.make_async_copy(
            ins[t].at[:, cols], rows_in.at[t, :, cols], in_sem.at[c, t, s]
        )

    def load_all(c):
        for t in range(4):
            for s in range(ways):
                load(c, t, s).start()

    load_all(0)
    barrier = pltpu.get_barrier_semaphore()

    @pl.loop(1, n)
    def _(i):
        pl.semaphore_signal(barrier, inc=1, device_id=peer(i)[1], device_id_type=MESH)

    def pack(c):
        for t in range(4):
            for s in range(ways):
                load(c, t, s).wait()
                part = rows_in[t, :, s * span + c * width : s * span + (c + 1) * width]
                part = dot(order[...], part, NN).astype(jnp.bfloat16)
                for g in range(groups):
                    stage[c, g * ways + s, t * rows : (t + 1) * rows, :] = part[
                        g * rows : (g + 1) * rows
                    ]

    def send_all(c):
        @pl.loop(1, n)
        def _(i):
            other, where = peer(i)
            pltpu.make_async_remote_copy(
                src_ref=stage.at[c, other],
                dst_ref=recv.at[c, me],
                send_sem=send_sem.at[c],
                recv_sem=recv_sem.at[c],
                device_id=where,
                device_id_type=MESH,
            ).start()

        recv[c, me] = stage[c, me]

    def return_all(c):
        @pl.loop(1, n)
        def _(i):
            other, where = peer(i)
            pltpu.make_async_remote_copy(
                src_ref=back.at[c, other],
                dst_ref=homes[c].at[me],
                send_sem=back_send_sem.at[c],
                recv_sem=back_recv_sem.at[c],
                device_id=where,
                device_id_type=MESH,
            ).start()

        pltpu.make_async_copy(back.at[c, me], homes[c].at[me], own_sem.at[c]).start()

    def wait_bytes(ref, sem):
        pltpu.make_async_copy(ref, ref, sem).wait()

    order[...] = block_order(dest_ref, groups, rows)
    for c in range(1, chunks):
        load_all(c)
    pack(0)
    pl.semaphore_wait(barrier, n - 1)
    send_all(0)
    for c in range(1, chunks):
        pack(c)
        send_all(c)

    zeros = jnp.sum(jnp.where(clip_ref[...] == 0, 1.0, 0.0), axis=1, keepdims=True)
    lane = lax.broadcasted_iota(jnp.int32, (8, seq), 1)
    sub = lax.broadcasted_iota(jnp.int32, (seq, 128), 0)
    lane_src, sub_src = lane // rows, sub // rows
    lane_pos, sub_pos = lane % rows, sub % rows
    for t in range(n):
        src = slot_ref[0, t]
        lane_pos = lane_pos + jnp.where(lane_src == src, t * rows, 0)
        sub_pos = sub_pos + jnp.where(sub_src == src, t * rows, 0)
    lane_clip = jnp.where(lane_pos.astype(jnp.float32) >= zeros, 1.0, 0.0)[0:1]
    sub_clip = jnp.where(sub_pos.astype(jnp.float32) >= zeros, 1.0, 0.0)[:, 0:1]
    bias[...] = jnp.where(lane_clip == sub_clip, 0.0, -1e30)
    gstage[...] = jnp.zeros_like(gstage)

    hd = qgain_ref.shape[1]
    scale = hd ** (-0.5)
    gain_q = qgain_ref[...]
    gain_k = kgain_ref[...]

    def head_of(c, h):
        cols = pl.ds(pl.multiple_of(h * hd, hd), hd)

        def take(t):
            return recv[c, :, t * rows : (t + 1) * rows, cols].reshape(seq, hd)

        gq = take(0).astype(jnp.float32)
        gk = take(1).astype(jnp.float32)
        gv = take(2)
        gdo = take(3)
        rq = lax.rsqrt(jnp.mean(gq * gq, axis=-1, keepdims=True) + EPS)
        rk = lax.rsqrt(jnp.mean(gk * gk, axis=-1, keepdims=True) + EPS)
        qn = (gq * rq * gain_q).astype(jnp.bfloat16)
        kn = (gk * rk * gain_k).astype(jnp.bfloat16)
        masked = dot(qn, kn, NT) * scale + bias[...]
        weights = jnp.exp(masked - jnp.max(masked, axis=-1, keepdims=True))
        probs = weights / jnp.sum(weights, axis=-1, keepdims=True)
        low = probs.astype(jnp.bfloat16)
        att = dot(low, gv, NN)
        dv = dot(low, gdo, TN)
        dp = dot(gdo, gv, NT)
        delta = jnp.sum(gdo.astype(jnp.float32) * att, axis=-1, keepdims=True)
        ds = (probs * (dp - delta) * scale).astype(jnp.bfloat16)
        dqn = dot(ds, kn, NN)
        dkn = dot(ds, qn, TN)
        mq = jnp.mean(gain_q * dqn * gq, axis=-1, keepdims=True)
        mk = jnp.mean(gain_k * dkn * gk, axis=-1, keepdims=True)
        dq = rq * gain_q * dqn - gq * (rq * rq * rq) * mq
        dk = rk * gain_k * dkn - gk * (rk * rk * rk) * mk
        gstage[:, 0:hd] += jnp.sum(dqn * gq * rq, axis=0, keepdims=True)
        gstage[:, hd : 2 * hd] += jnp.sum(dkn * gk * rk, axis=0, keepdims=True)
        for t, res in enumerate((att, dq, dk, dv)):
            back[c, :, t * rows : (t + 1) * rows, cols] = res.astype(jnp.bfloat16).reshape(
                n, rows, hd
            )

    for c in range(chunks):
        wait_bytes(recv.at[c, pl.ds(0, n - 1)], recv_sem.at[c])

        @pl.loop(0, heads)
        def _(h):
            head_of(c, h)

        if c == chunks - 1:
            @pl.loop(1, n)
            def _(i):
                pltpu.make_async_remote_copy(
                    src_ref=gstage,
                    dst_ref=grecv.at[me],
                    send_sem=gain_send_sem,
                    recv_sem=gain_recv_sem,
                    device_id=peer(i)[1],
                    device_id_type=MESH,
                ).start()

            grecv[me] = gstage[...]
        return_all(c)

    for c in range(chunks):
        wait_bytes(homes[c].at[pl.ds(0, n - 1)], back_recv_sem.at[c])
    wait_bytes(grecv.at[pl.ds(0, n - 1)], gain_recv_sem)
    for c in range(chunks):
        wait_bytes(stage.at[c, pl.ds(0, n - 1)], send_sem.at[c])
        wait_bytes(back.at[c, pl.ds(0, n - 1)], back_send_sem.at[c])
        pltpu.make_async_copy(back.at[c, me], homes[c].at[me], own_sem.at[c]).wait()
    wait_bytes(grecv.at[pl.ds(0, n - 1)], gain_send_sem)


def shards_fused(
    query_rows,
    key_rows,
    value_rows,
    output_grad,
    query_gain,
    key_gain,
    dest_groups,
    slot_sources,
    clip_index,
):
    groups = lax.axis_size("dp")
    ways = lax.axis_size("seq")
    n = groups * ways
    tok, full = query_rows.shape
    hd = query_gain.shape[0]
    rows = tok // groups
    heads_here = full // hd // ways
    heads = 2 if heads_here % 2 == 0 else 1
    chunks = heads_here // heads
    width = heads * hd
    seq = tok * ways
    factor = float(tok * n * (full // hd)) ** (-0.5)
    dims = (groups, ways, rows, chunks, width, heads)
    vmem = pl.BlockSpec(memory_space=pltpu.VMEM)
    smem = pl.BlockSpec(memory_space=pltpu.SMEM)
    slab = (n, 4 * rows, width)
    bf = jnp.bfloat16
    out = jax.ShapeDtypeStruct((tok, full), bf)
    dma = pltpu.SemaphoreType.DMA
    hbm = pl.BlockSpec(memory_space=pl.ANY)
    landed = pl.pallas_call(
        functools.partial(fused_kernel, dims),
        out_shape=[jax.ShapeDtypeStruct((n, 1, 2 * hd), jnp.float32)]
        + [jax.ShapeDtypeStruct(slab, bf)] * chunks,
        in_specs=[smem, smem] + [vmem] * 3 + [hbm] * 4,
        out_specs=[vmem] + [hbm] * chunks,
        scratch_shapes=[
            pltpu.VMEM((chunks,) + slab, bf),
            pltpu.VMEM((chunks,) + slab, bf),
            pltpu.VMEM((chunks,) + slab, bf),
            pltpu.VMEM((seq, seq), jnp.float32),
            pltpu.VMEM((1, 2 * hd), jnp.float32),
            pltpu.VMEM((tok, tok), bf),
            pltpu.VMEM((4, tok, full), bf),
            dma((chunks, 4, ways)),
            dma((chunks,)),
            dma((chunks,)),
            dma((chunks,)),
            dma((chunks,)),
            dma((chunks,)),
            dma,
            dma,
        ],
        compiler_params=pltpu.CompilerParams(
            collective_id=0, has_side_effects=True, vmem_limit_bytes=60 * 2**20
        ),
    )(
        dest_groups,
        slot_sources,
        clip_index,
        query_gain.reshape(1, hd),
        key_gain.reshape(1, hd),
        query_rows,
        key_rows,
        value_rows,
        output_grad,
    )
    return pl.pallas_call(
        functools.partial(home_kernel, dims, factor),
        out_shape=(out, out, out, out, jax.ShapeDtypeStruct((2, hd), jnp.float32)),
        in_specs=[smem, vmem] + [hbm] * chunks,
        out_specs=(hbm,) * 4 + (vmem,),
        scratch_shapes=[
            pltpu.VMEM((4, tok, full), bf),
            dma((4,)),
            pltpu.VMEM((chunks,) + slab, bf),
            dma((chunks,)),
        ],
        compiler_params=pltpu.CompilerParams(vmem_limit_bytes=60 * 2**20),
    )(dest_groups, *landed)


def shards(query_rows, *rest):
    if (query_rows.shape[0] // lax.axis_size("dp")) % 16 == 0:
        return shards_fused(query_rows, *rest)
    return shards_plain(query_rows, *rest)


def solution(mesh):
    return jax.shard_map(
        shards,
        mesh=mesh,
        in_specs=(
            P(("dp", "seq"), None),
            P(("dp", "seq"), None),
            P(("dp", "seq"), None),
            P(("dp", "seq"), None),
            P(),
            P(),
            P(("dp", "seq"), None),
            P("dp", None),
            P("dp", None),
        ),
        out_specs=(
            P(("dp", "seq"), None),
            P(("dp", "seq"), None),
            P(("dp", "seq"), None),
            P(("dp", "seq"), None),
            P(),
        ),
        check_vma=False,
    )
```
